32 devices in a mesh: parts: 2 (over x), head: 8 (over z, y), req: 2 (over core).
Axes of the slice: x: 2, y: 2, z: 4, core: 2. Of those that a mesh axis runs over, the one named last changes fastest.
Arguments:
- latent_cache: bfloat16 [16, 2048, 576], P(('parts', 'req'), 'head'), parts along dimension 0, may hold values from -8.5 to 8.5
- lengths: int32 [16], P('parts'), parts along dimension 0, may hold values from 170 to 2048, as said below
- slot_request: int32 [16], P('parts'), parts along dimension 0, may hold values from 0 to 7, each once
- queries: bfloat16 [4, 16, 16, 32, 192], P(None, ('parts', 'req'), None, 'head'), parts along dimension 1, may hold values from -64 to 64
- new_latent: bfloat16 [4, 16, 16, 576], P(None, ('parts', 'req')), parts along dimension 1, may hold values from -6 to 6
- key_up: bfloat16 [32, 128, 512], P('head'), may hold values from -0.25 to 0.25
- value_up: bfloat16 [32, 512, 128], P('head'), may hold values from -2 to 2
- output_weight: bfloat16 [32, 128, 7168], P('head'), may hold values from -0.09375 to 0.09375
Outputs:
- attended_out: bfloat16 [64, 16, 7168], P('head', ('parts', 'req')), parts along dimension 1
The draws below stay inside these ranges and needn't reach their ends.
There are 2 independent parts, one for each index of `parts`. The reference program is written for one: setup_inputs(seed, part) draws one part's arguments, and reference() takes and returns one part's arrays. A program takes and returns all parts, laid end to end along the dimension named above; an argument that names none is the same for every part. Nothing has to cross between parts.
Inputs may be any that keep to these rules, and one draw needn't show every extreme that they name: `lengths`: slots at or beyond a request's length are unused; one request has exactly 2048 and one exactly 170. `slot_request`: decode slots g * 4 to (g + 1) * 4 - 1 form decode group g; every request is served by exactly one slot.
All inputs are finite; a program needn't handle non-finite values.
Results may differ from the reference program's by a relative error of at most 0.014.
Values may be sent and summed in bfloat16 or wider, within the bound.
A program may use at most 128 MiB of HBM per device.

```python
import jax
import jax.numpy as jnp
from jax import lax

D = 7168
HEADS = 32
LATENT = 512
ROPE = 64
NOPE = 128
VHEAD = 128
CTX = 2048
REQS = 8
CONT = 16
STEPS = 4


def draw_latent_cache(key, part):
    key = jax.random.fold_in(key, 11)
    values = jnp.clip(jax.random.normal(key, (REQS, CTX, LATENT + ROPE), jnp.float32), -6.0, 6.0)
    return values.astype(jnp.bfloat16)


def draw_queries(key, part):
    key = jax.random.fold_in(key, 12)
    values = jnp.clip(1.5 * jax.random.normal(key, (STEPS, REQS, CONT, HEADS, NOPE + ROPE), jnp.float32), -9.0, 9.0)
    return values.astype(jnp.bfloat16)


def draw_lengths(key, part):
    key = jax.random.fold_in(key, 13)
    first_key, second_key = jax.random.split(key)
    drawn = jax.random.randint(first_key, (REQS,), CTX // 12, CTX + 1, jnp.int32)
    order = jax.random.permutation(second_key, REQS)
    drawn = drawn.at[order[0]].set(CTX)
    drawn = drawn.at[order[1]].set(CTX // 12)
    return drawn


def block_scale(rng, extent, cuts, low, high):
    def one(dim, blocks):
        draws = jax.random.uniform(jax.random.fold_in(jax.random.fold_in(rng, 6), dim), (blocks,), jnp.float32, low / len(cuts), high / len(cuts))
        return jnp.repeat(jnp.exp(draws), extent[dim] // blocks).reshape((-1,) + (1,) * (len(extent) - dim - 1))

    level = one(*cuts[0])
    for cut in cuts[1:]:
        level = level * one(*cut)
    return level


def noise(key, dims, spread, reach, cuts=(), kind=jnp.bfloat16):
    values = spread * jax.random.normal(key, dims, jnp.float32)
    if cuts:
        values = values * block_scale(key, dims, cuts, -0.22, 0.18)
    return jnp.clip(values, -reach, reach).astype(kind)


def setup_inputs(seed: int = 0, part: int = 0) -> dict:
    key_list = jax.random.split(jax.random.key(seed), 9)
    part_keys = jax.random.split(jax.random.fold_in(key_list[8], part), 9)
    return {
        "latent_cache": draw_latent_cache(jax.random.fold_in(jax.random.fold_in(key_list[8], part), 71), part),
        "lengths": draw_lengths(jax.random.fold_in(jax.random.fold_in(key_list[8], part), 71), part),
        "slot_request": jax.random.permutation(part_keys[2], REQS).astype(jnp.int32),
        "queries": draw_queries(jax.random.fold_in(jax.random.fold_in(key_list[8], part), 71), part),
        "new_latent": noise(part_keys[4], (STEPS, REQS, CONT, LATENT + ROPE), 1.0, 6.0, ((1, 2),)),
        "key_up": noise(key_list[5], (HEADS, NOPE, LATENT), LATENT ** -0.5, 0.25, ((0, 8),)),
        "value_up": noise(key_list[6], (HEADS, LATENT, VHEAD), (max(LATENT // 64, 1)) ** -0.5, 2.0, ((0, 8),)),
        "output_weight": noise(key_list[7], (HEADS, VHEAD, D), (HEADS * VHEAD) ** -0.5, 0.09375, ((0, 8),)),
    }


def rounded(values):
    return lax.optimization_barrier(values.astype(jnp.bfloat16)).astype(jnp.float32)


def reference(latent_cache, lengths, slot_request, queries, new_latent, key_up, value_up, output_weight):
    score_scale = (NOPE + ROPE) ** -0.5
    absorbed = jnp.einsum('tschd,hdk->tschk', queries[..., :NOPE].astype(jnp.float32), key_up.astype(jnp.float32))
    full_query = jnp.concatenate([rounded(absorbed), queries[..., NOPE:].astype(jnp.float32)], axis=-1)
    value_full = value_up.astype(jnp.float32)
    output_full = output_weight.astype(jnp.float32)
    places = jnp.arange(CTX, dtype=jnp.int32)
    causal = jnp.arange(STEPS)[:, None] >= jnp.arange(STEPS)[None, :]

    def per_slot(slot):
        request = slot_request[slot]
        cache_rows = lax.dynamic_index_in_dim(latent_cache, request, 0, keepdims=False).astype(jnp.float32)
        prompt_length = lax.dynamic_index_in_dim(lengths, request, 0, keepdims=False)
        query_grid = lax.dynamic_index_in_dim(full_query, slot, 1, keepdims=False)
        own_latent = lax.dynamic_index_in_dim(new_latent, slot, 1, keepdims=False).astype(jnp.float32)
        usable = (places < prompt_length)[None, None, None, :]
        own_mask = causal[:, None, None, :]
        cache_scores = jnp.einsum('tchk,pk->tchp', query_grid, cache_rows) * score_scale
        cache_scores = jnp.where(usable, cache_scores, -1e30)
        own_scores = jnp.einsum('tchk,uck->tchu', query_grid, own_latent) * score_scale
        own_scores = jnp.where(own_mask, own_scores, -1e30)
        highest = jnp.maximum(jnp.max(cache_scores, axis=-1), jnp.max(own_scores, axis=-1))
        cache_weights = jnp.where(usable, jnp.exp(cache_scores - highest[..., None]), 0.0)
        own_weights = jnp.where(own_mask, jnp.exp(own_scores - highest[..., None]), 0.0)
        denominator = jnp.sum(cache_weights, axis=-1) + jnp.sum(own_weights, axis=-1)
        weighted = jnp.einsum('tchp,pk->tchk', rounded(cache_weights), cache_rows[:, :LATENT])
        weighted = weighted + jnp.einsum('tchu,uck->tchk', rounded(own_weights), own_latent[..., :LATENT])
        attended = rounded(weighted / denominator[..., None])
        head_out = rounded(jnp.einsum('tchk,hkd->tchd', attended, value_full))
        summed = jnp.einsum('tchd,hdo->tco', head_out, output_full)
        return summed.reshape(STEPS * CONT, D)

    result = lax.map(per_slot, jnp.arange(REQS, dtype=jnp.int32))
    return jnp.transpose(result, (1, 0, 2)).astype(jnp.bfloat16)
```

```python
import functools

import jax
import jax.numpy as jnp
from jax import lax
from jax.experimental import pallas as pl
from jax.experimental.pallas import tpu as pltpu
from jax.sharding import PartitionSpec as P

MESH = pl.DeviceIdType.MESH
F32 = jnp.float32
BF16 = jnp.bfloat16
LOW = -1e30


def dot_nt(a, b):
    return lax.dot_general(a, b, (((1,), (1,)), ((), ())), preferred_element_type=F32)


def attend(state, absorbed, rotary, keys, rope, mask, scale):
    top, total, acc = state
    scores = (dot_nt(absorbed, keys) + dot_nt(rotary, rope)) * scale
    scores = jnp.where(mask, scores, LOW)
    new_top = jnp.maximum(top, jnp.max(scores, axis=1, keepdims=True))
    weights = jnp.where(mask, jnp.exp(scores - new_top), 0.0)
    rescale = jnp.exp(top - new_top)
    total = total * rescale + jnp.sum(weights, axis=1, keepdims=True)
    acc = acc * rescale + jnp.dot(weights.astype(BF16), keys, preferred_element_type=F32)
    return new_top, total, acc


def own_mask(rows, steps, cont, heads):
    row = lax.broadcasted_iota(jnp.int32, (rows, steps * cont), 0) % (steps * cont)
    col = lax.broadcasted_iota(jnp.int32, (rows, steps * cont), 1)
    return (row % cont == col % cont) & (col // cont <= row // cont)


def attention_kernel(
    scale, steps, cont,
    anchor_ref, source_ref, length_ref,
    cache_ref, query_ref, own_ref, up_ref, value_ref, out_ref,
    full_ref, top_ref, total_ref, acc_ref,
):
    slot = pl.program_id(0)
    heads, tokens, nope = query_ref.shape[1], query_ref.shape[2], up_ref.shape[1]
    stripes, span = cache_ref.shape[0], cache_ref.shape[3]
    latent = up_ref.shape[2]
    rows = heads * tokens
    length = length_ref[slot]
    for h in range(heads):
        q = query_ref[0, h]
        full_ref[pl.ds(h * tokens, tokens), :latent] = jnp.dot(
            q[:, :nope], up_ref[h], preferred_element_type=F32
        ).astype(BF16)
        full_ref[pl.ds(h * tokens, tokens), latent:] = q[:, nope:]
    zero = (jnp.full((rows, 1), LOW, F32), jnp.zeros((rows, 1), F32), jnp.zeros((rows, latent), F32))
    own = own_ref[0]
    state = attend(
        zero, full_ref[:, :latent], full_ref[:, latent:], own[:, :latent], own[:, latent:],
        own_mask(rows, steps, cont, heads), scale,
    )
    top_ref[...], total_ref[...], acc_ref[...] = state
    for stripe in range(stripes):
        @pl.when(stripe * span < length)
        def _():
            block = cache_ref[stripe, 0, 0]
            place = stripe * span + lax.broadcasted_iota(jnp.int32, (rows, span), 1)
            state = attend(
                (top_ref[...], total_ref[...], acc_ref[...]),
                full_ref[:, :latent], full_ref[:, latent:], block[:, :latent], block[:, latent:],
                place < length, scale,
            )
            top_ref[...], total_ref[...], acc_ref[...] = state
    attended = (acc_ref[...] / total_ref[...]).astype(BF16)
    width = value_ref.shape[2]
    for h in range(heads):
        out_ref[0, :, h * width:(h + 1) * width] = jnp.dot(
            attended[h * tokens:(h + 1) * tokens], value_ref[h], preferred_element_type=F32
        ).astype(BF16)


def project_kernel(
    chunk, rows_ref, weight_ref, out_ref,
    outbox, inbox, middle, landed, send_a, recv_a, send_b, recv_b,
):
    count = lax.axis_size("head")
    half = count // 2
    me = lax.axis_index("head")
    mine, odd = me // 2, me % 2
    partner = me + 1 - 2 * odd
    size = out_ref.shape[0]
    chunks = weight_ref.shape[1] // chunk
    barrier = pltpu.get_barrier_semaphore()
    pl.semaphore_signal(barrier, inc=1, device_id={"head": partner}, device_id_type=MESH)
    for i in range(1, half):
        peer = lax.rem(mine + i, half) * 2 + odd
        pl.semaphore_signal(barrier, inc=1, device_id={"head": peer}, device_id_type=MESH)
    pl.semaphore_wait(barrier, half)

    firsts = []
    for c in range(chunks):
        cols = slice(c * chunk, (c + 1) * chunk)
        outbox[c] = jnp.dot(
            rows_ref[1 - odd], weight_ref[:, cols], preferred_element_type=F32
        ).astype(BF16)
        copy = pltpu.make_async_remote_copy(
            src_ref=outbox.at[c], dst_ref=inbox.at[c], send_sem=send_a.at[c], recv_sem=recv_a.at[c],
            device_id={"head": partner}, device_id_type=MESH,
        )
        copy.start()
        firsts.append(copy)
    seconds = []
    for c in range(chunks):
        cols = slice(c * chunk, (c + 1) * chunk)
        product = jnp.dot(rows_ref[odd], weight_ref[:, cols], preferred_element_type=F32)
        firsts[c].wait_recv()
        total = (product + inbox[c].astype(F32)).astype(BF16)
        for k in range(half):
            middle[c, k] = total[k * size:(k + 1) * size]
        for i in range(1, half):
            k = lax.rem(mine + i, half)
            copy = pltpu.make_async_remote_copy(
                src_ref=middle.at[c, k], dst_ref=landed.at[c, i],
                send_sem=send_b.at[c, i], recv_sem=recv_b.at[c, i],
                device_id={"head": k * 2 + odd}, device_id_type=MESH,
            )
            copy.start()
            seconds.append(copy)
    for c in range(chunks):
        total = middle[c, mine].astype(F32)
        for i in range(1, half):
            seconds[c * (half - 1) + i - 1].wait_recv()
            total = total + landed[c, i].astype(F32)
        out_ref[:, c * chunk:(c + 1) * chunk] = total.astype(BF16)
    for copy in firsts + seconds:
        copy.wait_send()


def project(head_out, output_weight):
    count = lax.axis_size("head")
    half = count // 2
    slots, tokens, depth = head_out.shape
    width = output_weight.shape[2]
    per = tokens // count
    size = per * slots
    chunk = 1024 if width % 1024 == 0 else width
    chunks = width // chunk
    rows = jnp.transpose(head_out.reshape(slots, half, 2, per, depth), (2, 1, 3, 0, 4))
    rows = rows.reshape(2, half * size, depth)
    vmem = pl.BlockSpec(memory_space=pltpu.VMEM)
    out = pl.pallas_call(
        functools.partial(project_kernel, chunk),
        out_shape=jax.ShapeDtypeStruct((size, width), BF16),
        in_specs=[vmem, vmem],
        out_specs=vmem,
        scratch_shapes=[
            pltpu.VMEM((chunks, half * size, chunk), BF16),
            pltpu.VMEM((chunks, half * size, chunk), BF16),
            pltpu.VMEM((chunks, half, size, chunk), BF16),
            pltpu.VMEM((chunks, half, size, chunk), BF16),
            pltpu.SemaphoreType.DMA((chunks,)),
            pltpu.SemaphoreType.DMA((chunks,)),
            pltpu.SemaphoreType.DMA((chunks, half)),
            pltpu.SemaphoreType.DMA((chunks, half)),
        ],
        compiler_params=pltpu.CompilerParams(
            collective_id=1, has_side_effects=True, vmem_limit_bytes=48 * 1024 * 1024
        ),
        cost_estimate=pl.CostEstimate(
            flops=4 * half * size * depth * width, bytes_accessed=2 * depth * width, transcendentals=0
        ),
    )(rows, output_weight.reshape(depth, width))
    return out.reshape(per, slots, width)


def shards(
    latent_cache, lengths, slot_request, queries, new_latent, key_up, value_up, output_weight
):
    slots, span, cache_width = latent_cache.shape
    nope, latent = key_up.shape[1], key_up.shape[2]
    steps, _, cont, heads, query_width = queries.shape
    vhead = value_up.shape[2]
    tokens = steps * cont
    rows = tokens * heads
    scale = (nope + cache_width - latent) ** (-0.5)
    group = lax.axis_index("req")
    stripes, groups = lax.axis_size("head"), lax.axis_size("req")
    my_requests = lax.dynamic_slice_in_dim(slot_request, group * slots, slots)
    matches = my_requests[:, None] == jnp.arange(lengths.shape[0], dtype=jnp.int32)[None, :]
    my_lengths = jnp.sum(jnp.where(matches, lengths[None, :], 0), axis=1)
    query_rows = jnp.transpose(queries, (1, 3, 0, 2, 4)).reshape(slots, heads, tokens, query_width)
    own_rows = jnp.transpose(new_latent, (1, 0, 2, 3)).reshape(slots, tokens, cache_width)
    gathered = lax.all_gather(latent_cache[None], ("head", "req"), axis=0, tiled=True)
    gathered = gathered.reshape(stripes, groups, slots, span, cache_width)
    head_out = pl.pallas_call(
        functools.partial(attention_kernel, scale, steps, cont),
        out_shape=jax.ShapeDtypeStruct((slots, tokens, heads * vhead), BF16),
        grid_spec=pltpu.PrefetchScalarGridSpec(
            num_scalar_prefetch=3,
            grid=(slots,),
            in_specs=[
                pl.BlockSpec((stripes, 1, 1, span, cache_width), lambda s, a, i, l: (0, a[s], i[s], 0, 0)),
                pl.BlockSpec((1, heads, tokens, query_width), lambda s, a, i, l: (s, 0, 0, 0)),
                pl.BlockSpec((1, tokens, cache_width), lambda s, a, i, l: (s, 0, 0)),
                pl.BlockSpec((heads, nope, latent), lambda s, a, i, l: (0, 0, 0)),
                pl.BlockSpec((heads, latent, vhead), lambda s, a, i, l: (0, 0, 0)),
            ],
            out_specs=pl.BlockSpec((1, tokens, heads * vhead), lambda s, a, i, l: (s, 0, 0)),
            scratch_shapes=[
                pltpu.VMEM((rows, cache_width), BF16),
                pltpu.VMEM((rows, 1), F32),
                pltpu.VMEM((rows, 1), F32),
                pltpu.VMEM((rows, latent), F32),
            ],
        ),
        compiler_params=pltpu.CompilerParams(vmem_limit_bytes=40 * 1024 * 1024),
    )(my_requests // slots, my_requests % slots, my_lengths, gathered, query_rows, own_rows, key_up, value_up)
    return project(head_out, output_weight)


def solution(mesh):
    in_specs = (
        P(("parts", "req"), "head", None),
        P("parts"),
        P("parts"),
        P(None, ("parts", "req"), None, "head", None),
        P(None, ("parts", "req"), None, None),
        P("head", None, None),
        P("head", None, None),
        P("head", None, None),
    )
    out_specs = P("head", ("parts", "req"), None)
    return jax.shard_map(shards, mesh=mesh, in_specs=in_specs, out_specs=out_specs, check_vma=False)
```

```python
import functools

import jax
import jax.numpy as jnp
from jax import lax
from jax.experimental import pallas as pl
from jax.experimental.pallas import tpu as pltpu
from jax.sharding import PartitionSpec as P

MESH = pl.DeviceIdType.MESH
F32 = jnp.float32
BF16 = jnp.bfloat16
LOW = -1e30


def dot_nt(a, b):
    return lax.dot_general(a, b, (((1,), (1,)), ((), ())), preferred_element_type=F32)


def attend(state, absorbed, rotary, keys, rope, mask, scale):
    top, total, acc = state
    scores = (dot_nt(absorbed, keys) + dot_nt(rotary, rope)) * scale
    scores = jnp.where(mask, scores, LOW)
    new_top = jnp.maximum(top, jnp.max(scores, axis=1, keepdims=True))
    weights = jnp.where(mask, jnp.exp(scores - new_top), 0.0)
    rescale = jnp.exp(top - new_top)
    total = total * rescale + jnp.sum(weights, axis=1, keepdims=True)
    acc = acc * rescale + jnp.dot(weights.astype(BF16), keys, preferred_element_type=F32)
    return new_top, total, acc


def own_mask(rows, steps, cont, heads):
    row = lax.broadcasted_iota(jnp.int32, (rows, steps * cont), 0) % (steps * cont)
    col = lax.broadcasted_iota(jnp.int32, (rows, steps * cont), 1)
    return (row % cont == col % cont) & (col // cont <= row // cont)


def attention_kernel(
    scale, steps, cont,
    request_ref, length_ref, cache_ref, query_ref, rotary_ref, own_ref, up_ref, value_ref, out_ref,
    both, blocks, full, top_ref, total_ref, acc_ref, kept, kept_top, kept_total,
    partial, partial_in, stats, stats_in,
    swap_send, swap_recv, query_send, query_recv, right_send, right_recv, left_send, left_recv,
    partial_send, partial_recv, stats_send, stats_recv,
):
    slots, heads, tokens, nope = query_ref.shape
    latent, rope_width = up_ref.shape[2], rotary_ref.shape[2]
    width = value_ref.shape[2]
    groups = latent // rope_width
    span = cache_ref.shape[1] * groups // (groups + 1)
    rows = heads * tokens
    half = lax.axis_size("head") // 2
    me = lax.axis_index("head")
    mine, odd = me // 2, me % 2
    partner, right, left = me + 1 - 2 * odd, me + 2, me - 2
    group = lax.axis_index("req")
    not_first, not_last = mine > 0, mine < half - 1

    barrier = pltpu.get_barrier_semaphore()
    pl.semaphore_signal(barrier, inc=1, device_id={"req": 1 - group}, device_id_type=MESH)
    pl.semaphore_signal(barrier, inc=1, device_id={"head": partner}, device_id_type=MESH)

    @pl.when(not_last)
    def _():
        pl.semaphore_signal(barrier, inc=1, device_id={"head": right}, device_id_type=MESH)

    @pl.when(not_first)
    def _():
        pl.semaphore_signal(barrier, inc=1, device_id={"head": left}, device_id_type=MESH)

    pl.semaphore_wait(barrier, 4 - (mine == 0).astype(jnp.int32) - (mine == half - 1).astype(jnp.int32))

    def swap():
        return pltpu.make_async_remote_copy(
            src_ref=cache_ref, dst_ref=both.at[group], send_sem=swap_send, recv_sem=swap_recv,
            device_id={"req": 1 - group}, device_id_type=MESH,
        )

    def swap_in():
        return pltpu.make_async_remote_copy(
            src_ref=cache_ref, dst_ref=both.at[1 - group], send_sem=swap_send, recv_sem=swap_recv,
            device_id={"req": 1 - group}, device_id_type=MESH,
        )

    def to_partner(source, target, send, recv, slot):
        return pltpu.make_async_remote_copy(
            src_ref=source, dst_ref=target, send_sem=send.at[slot], recv_sem=recv.at[slot],
            device_id={"head": partner}, device_id_type=MESH,
        )

    def send_query(slot):
        return to_partner(full.at[slot, 0], full.at[slot, 1], query_send, query_recv, slot)

    def send_partial(slot):
        return to_partner(partial.at[slot], partial_in.at[slot], partial_send, partial_recv, slot)

    def send_stats(slot):
        return to_partner(stats.at[slot], stats_in.at[slot], stats_send, stats_recv, slot)

    def along(slot, step, block, send, recv, device):
        return pltpu.make_async_remote_copy(
            src_ref=blocks.at[slot, block], dst_ref=blocks.at[slot, block],
            send_sem=send.at[slot, step], recv_sem=recv.at[slot, step],
            device_id={"head": device}, device_id_type=MESH,
        )

    def rightward(slot, step, block):
        return along(slot, step, block, right_send, right_recv, right)

    def leftward(slot, step, block):
        return along(slot, step, block, left_send, left_recv, left)

    def send_right(slot, step):
        @pl.when(not_last & (mine - step >= 0))
        def _():
            rightward(slot, step, mine - step).start()

    def send_left(slot, step):
        @pl.when(not_first & (mine + step < half))
        def _():
            leftward(slot, step, mine + step).start()

    swap().start()
    both[group] = cache_ref[...]

    @pl.loop(0, slots)
    def _(slot):
        for h in range(heads):
            full[slot, 0, h * tokens:(h + 1) * tokens, :latent] = jnp.dot(
                query_ref[slot, h], up_ref[h], preferred_element_type=F32
            ).astype(BF16)
        full[slot, 0, :, latent:latent + rope_width] = rotary_ref[slot]
        full[slot, 0, :, latent + rope_width:] = jnp.zeros(
            (rows, full.shape[3] - latent - rope_width), BF16
        )
        send_query(slot).start()

    swap_in().wait_recv()

    @pl.loop(0, slots)
    def _(slot):
        request = request_ref[slot]
        blocks[slot, mine] = both[request // slots, request % slots]

    for slot in range(min(2, slots)):
        send_right(slot, 0)
        send_left(slot, 0)

    generated = own_mask(2 * rows, steps, cont, heads)
    generated = generated & (lax.broadcasted_iota(jnp.int32, generated.shape, 0) < rows)

    def merge(slot):
        send_partial(slot).wait_recv()
        send_stats(slot).wait_recv()
        other_top, other_total = stats_in[slot, :, :1], stats_in[slot, :, 64:65]
        top = jnp.maximum(kept_top[slot], other_top)
        here = jnp.exp(kept_top[slot] - top)
        there = jnp.exp(other_top - top) * other_total
        total = kept_total[slot] * here + there
        attended = (kept[slot] * here + partial_in[slot].astype(F32) * there) / total
        attended = attended.astype(BF16)
        for h in range(heads):
            out_ref[slot, :, h * width:(h + 1) * width] = jnp.dot(
                attended[h * tokens:(h + 1) * tokens], value_ref[h], preferred_element_type=F32
            ).astype(BF16)

    @pl.loop(0, slots)
    def _(slot):
        length = length_ref[slot]

        def absorb(block):
            keys = blocks[slot, block, :span]
            packed = blocks[slot, block, span:]
            rope = jnp.concatenate(
                [packed[:, g * rope_width:(g + 1) * rope_width] for g in range(groups)], axis=0
            )
            stripe = block * 2 + odd
            place = stripe * span + lax.broadcasted_iota(jnp.int32, (2 * rows, span), 1)
            query = full[slot].reshape(2 * rows, full.shape[3])
            state = attend(
                (top_ref[...], total_ref[...], acc_ref[...]),
                query[:, :latent], query[:, latent:latent + rope_width], keys, rope,
                place < length, scale,
            )
            top_ref[...], total_ref[...], acc_ref[...] = state

        send_query(slot).wait_recv()
        query = full[slot].reshape(2 * rows, full.shape[3])
        own = own_ref[slot]
        zero = (
            jnp.full((2 * rows, 1), LOW, F32),
            jnp.zeros((2 * rows, 1), F32),
            jnp.zeros((2 * rows, latent), F32),
        )
        state = attend(
            zero, query[:, :latent], query[:, latent:latent + rope_width],
            own[:, :latent], own[:, latent:], generated, scale,
        )
        top_ref[...], total_ref[...], acc_ref[...] = state
        absorb(mine)
        for step in range(half - 1):
            from_left, from_right = mine - 1 - step >= 0, mine + 1 + step < half

            @pl.when(from_left)
            def _():
                rightward(slot, step, mine - 1 - step).wait_recv()

            if step + 1 < half - 1:
                send_right(slot, step + 1)

            @pl.when(from_right)
            def _():
                leftward(slot, step, mine + 1 + step).wait_recv()

            if step + 1 < half - 1:
                send_left(slot, step + 1)

            @pl.when(from_left)
            def _():
                absorb(mine - 1 - step)

            @pl.when(from_right)
            def _():
                absorb(mine + 1 + step)

        @pl.when(slot + 2 < slots)
        def _():
            send_right(slot + 2, 0)
            send_left(slot + 2, 0)

        total = total_ref[rows:]
        partial[slot] = (acc_ref[rows:] / jnp.where(total > 0.0, total, 1.0)).astype(BF16)
        lane = lax.broadcasted_iota(jnp.int32, (rows, 128), 1)
        stats[slot] = jnp.where(lane < 64, top_ref[rows:], total)
        send_partial(slot).start()
        send_stats(slot).start()
        kept[slot] = acc_ref[:rows]
        kept_top[slot] = top_ref[:rows]
        kept_total[slot] = total_ref[:rows]

        @pl.when(slot > 0)
        def _():
            merge(slot - 1)

    merge(slots - 1)

    swap().wait_send()

    @pl.loop(0, slots)
    def _(slot):
        send_query(slot).wait_send()
        send_partial(slot).wait_send()
        send_stats(slot).wait_send()
        for step in range(half - 1):
            @pl.when(not_last & (mine - step >= 0))
            def _():
                rightward(slot, step, mine - step).wait_send()

            @pl.when(not_first & (mine + step < half))
            def _():
                leftward(slot, step, mine + step).wait_send()


def project_kernel(
    chunk, rows_ref, weight_ref, out_ref,
    outbox, inbox, middle, landed, send_a, recv_a, send_b, recv_b,
):
    count = lax.axis_size("head")
    half = count // 2
    me = lax.axis_index("head")
    mine, odd = me // 2, me % 2
    partner = me + 1 - 2 * odd
    size = out_ref.shape[0]
    chunks = weight_ref.shape[1] // chunk
    barrier = pltpu.get_barrier_semaphore()
    pl.semaphore_signal(barrier, inc=1, device_id={"head": partner}, device_id_type=MESH)
    for i in range(1, half):
        peer = lax.rem(mine + i, half) * 2 + odd
        pl.semaphore_signal(barrier, inc=1, device_id={"head": peer}, device_id_type=MESH)
    pl.semaphore_wait(barrier, half)

    firsts = []
    for c in range(chunks):
        cols = slice(c * chunk, (c + 1) * chunk)
        outbox[c] = jnp.dot(
            rows_ref[1 - odd], weight_ref[:, cols], preferred_element_type=F32
        ).astype(BF16)
        copy = pltpu.make_async_remote_copy(
            src_ref=outbox.at[c], dst_ref=inbox.at[c], send_sem=send_a.at[c], recv_sem=recv_a.at[c],
            device_id={"head": partner}, device_id_type=MESH,
        )
        copy.start()
        firsts.append(copy)
    seconds = []
    for c in range(chunks):
        cols = slice(c * chunk, (c + 1) * chunk)
        product = jnp.dot(rows_ref[odd], weight_ref[:, cols], preferred_element_type=F32)
        firsts[c].wait_recv()
        total = (product + inbox[c].astype(F32)).astype(BF16)
        for k in range(half):
            middle[c, k] = total[k * size:(k + 1) * size]
        for i in range(1, half):
            k = lax.rem(mine + i, half)
            copy = pltpu.make_async_remote_copy(
                src_ref=middle.at[c, k], dst_ref=landed.at[c, i],
                send_sem=send_b.at[c, i], recv_sem=recv_b.at[c, i],
                device_id={"head": k * 2 + odd}, device_id_type=MESH,
            )
            copy.start()
            seconds.append(copy)
    for c in range(chunks):
        total = middle[c, mine].astype(F32)
        for i in range(1, half):
            seconds[c * (half - 1) + i - 1].wait_recv()
            total = total + landed[c, i].astype(F32)
        out_ref[:, c * chunk:(c + 1) * chunk] = total.astype(BF16)
    for copy in firsts + seconds:
        copy.wait_send()


def project(head_out, output_weight):
    count = lax.axis_size("head")
    half = count // 2
    slots, tokens, depth = head_out.shape
    width = output_weight.shape[2]
    per = tokens // count
    size = per * slots
    chunk = 1024 if width % 1024 == 0 else width
    chunks = width // chunk
    rows = jnp.transpose(head_out.reshape(slots, half, 2, per, depth), (2, 1, 3, 0, 4))
    rows = rows.reshape(2, half * size, depth)
    vmem = pl.BlockSpec(memory_space=pltpu.VMEM)
    out = pl.pallas_call(
        functools.partial(project_kernel, chunk),
        out_shape=jax.ShapeDtypeStruct((size, width), BF16),
        in_specs=[vmem, vmem],
        out_specs=vmem,
        scratch_shapes=[
            pltpu.VMEM((chunks, half * size, chunk), BF16),
            pltpu.VMEM((chunks, half * size, chunk), BF16),
            pltpu.VMEM((chunks, half, size, chunk), BF16),
            pltpu.VMEM((chunks, half, size, chunk), BF16),
            pltpu.SemaphoreType.DMA((chunks,)),
            pltpu.SemaphoreType.DMA((chunks,)),
            pltpu.SemaphoreType.DMA((chunks, half)),
            pltpu.SemaphoreType.DMA((chunks, half)),
        ],
        compiler_params=pltpu.CompilerParams(
            collective_id=1, has_side_effects=True, vmem_limit_bytes=48 * 1024 * 1024
        ),
        cost_estimate=pl.CostEstimate(
            flops=4 * half * size * depth * width, bytes_accessed=2 * depth * width, transcendentals=0
        ),
    )(rows, output_weight.reshape(depth, width))
    return out.reshape(per, slots, width)


def shards(
    latent_cache, lengths, slot_request, queries, new_latent, key_up, value_up, output_weight
):
    slots, span, cache_width = latent_cache.shape
    nope, latent = key_up.shape[1], key_up.shape[2]
    steps, _, cont, heads, query_width = queries.shape
    vhead = value_up.shape[2]
    tokens = steps * cont
    rows = tokens * heads
    scale = (nope + cache_width - latent) ** (-0.5)
    group = lax.axis_index("req")
    stripes, groups = lax.axis_size("head"), lax.axis_size("req")
    my_requests = lax.dynamic_slice_in_dim(slot_request, group * slots, slots)
    matches = my_requests[:, None] == jnp.arange(lengths.shape[0], dtype=jnp.int32)[None, :]
    my_lengths = jnp.sum(jnp.where(matches, lengths[None, :], 0), axis=1)
    rope = cache_width - latent
    packs = latent // rope
    query_rows = jnp.transpose(queries, (1, 3, 0, 2, 4)).reshape(slots, heads, tokens, query_width)
    rotary_rows = query_rows[..., nope:].reshape(slots, rows, rope)
    own_rows = jnp.transpose(new_latent, (1, 0, 2, 3)).reshape(slots, tokens, cache_width)
    packed = latent_cache[..., latent:].reshape(slots, packs, span // packs, rope)
    packed = jnp.transpose(packed, (0, 2, 1, 3)).reshape(slots, span // packs, latent)
    cache_rows = jnp.concatenate([latent_cache[..., :latent], packed], axis=1)
    deep = span + span // packs
    vmem, smem = pl.BlockSpec(memory_space=pltpu.VMEM), pl.BlockSpec(memory_space=pltpu.SMEM)
    half = stripes // 2
    padded = -(-cache_width // 128) * 128
    dma = pltpu.SemaphoreType.DMA
    head_out = pl.pallas_call(
        functools.partial(attention_kernel, scale, steps, cont),
        out_shape=jax.ShapeDtypeStruct((slots, tokens, heads * vhead), BF16),
        in_specs=[smem, smem] + [vmem] * 6,
        out_specs=vmem,
        scratch_shapes=[
            pltpu.VMEM((groups, slots, deep, latent), BF16),
            pltpu.VMEM((slots, half, deep, latent), BF16),
            pltpu.VMEM((slots, 2, rows, padded), BF16),
            pltpu.VMEM((2 * rows, 1), F32),
            pltpu.VMEM((2 * rows, 1), F32),
            pltpu.VMEM((2 * rows, latent), F32),
            pltpu.VMEM((slots, rows, latent), F32),
            pltpu.VMEM((slots, rows, 1), F32),
            pltpu.VMEM((slots, rows, 1), F32),
            pltpu.VMEM((slots, rows, latent), BF16),
            pltpu.VMEM((slots, rows, latent), BF16),
            pltpu.VMEM((slots, rows, 128), F32),
            pltpu.VMEM((slots, rows, 128), F32),
            dma, dma, dma((slots,)), dma((slots,)),
            dma((slots, half - 1)), dma((slots, half - 1)), dma((slots, half - 1)), dma((slots, half - 1)),
            dma((slots,)), dma((slots,)), dma((slots,)), dma((slots,)),
        ],
        compiler_params=pltpu.CompilerParams(
            collective_id=2, has_side_effects=True, vmem_limit_bytes=48 * 1024 * 1024
        ),
        cost_estimate=pl.CostEstimate(
            flops=4 * slots * rows * stripes * span * latent,
            bytes_accessed=2 * slots * deep * latent,
            transcendentals=slots * rows * stripes * span,
        ),
    )(my_requests, my_lengths, cache_rows, query_rows[..., :nope], rotary_rows, own_rows, key_up, value_up)
    return project(head_out, output_weight)


def solution(mesh):
    in_specs = (
        P(("parts", "req"), "head", None),
        P("parts"),
        P("parts"),
        P(None, ("parts", "req"), None, "head", None),
        P(None, ("parts", "req"), None, None),
        P("head", None, None),
        P("head", None, None),
        P("head", None, None),
    )
    out_specs = P("head", ("parts", "req"), None)
    return jax.shard_map(shards, mesh=mesh, in_specs=in_specs, out_specs=out_specs, check_vma=False)
```

```python
import functools

import jax
import jax.numpy as jnp
from jax import lax
from jax.experimental import pallas as pl
from jax.experimental.pallas import tpu as pltpu
from jax.sharding import PartitionSpec as P

MESH = pl.DeviceIdType.MESH
F32 = jnp.float32
BF16 = jnp.bfloat16
LOW = -1e30


def dot_nt(a, b):
    return lax.dot_general(a, b, (((1,), (1,)), ((), ())), preferred_element_type=F32)


def attend(state, absorbed, rotary, keys, rope, mask, scale):
    top, total, acc = state
    scores = (dot_nt(absorbed, keys) + dot_nt(rotary, rope)) * scale
    scores = jnp.where(mask, scores, LOW)
    new_top = jnp.maximum(top, jnp.max(scores, axis=1, keepdims=True))
    weights = jnp.where(mask, jnp.exp(scores - new_top), 0.0)
    rescale = jnp.exp(top - new_top)
    total = total * rescale + jnp.sum(weights, axis=1, keepdims=True)
    acc = acc * rescale + jnp.dot(weights.astype(BF16), keys, preferred_element_type=F32)
    return new_top, total, acc


def own_mask(rows, steps, cont, per):
    tokens = steps * cont
    row = lax.broadcasted_iota(jnp.int32, (rows, tokens), 0) % tokens
    odd, rest = row // (tokens // 2), row % (tokens // 2)
    row = (2 * (rest // per) + odd) * per + rest % per
    col = lax.broadcasted_iota(jnp.int32, (rows, tokens), 1)
    return (row % cont == col % cont) & (col // cont <= row // cont)


def attention_kernel(
    scale, steps, cont,
    request_ref, length_ref, cache_ref, query_ref, rotary_ref, own_ref, up_ref, value_ref, weight_hbm, out_ref,
    both, blocks, full, top_ref, total_ref, acc_ref, kept, kept_top, kept_total,
    partial, partial_in, stats, stats_in,
    swap_send, swap_recv, query_send, query_recv, right_send, right_recv, left_send, left_recv,
    partial_send, partial_recv, stats_send, stats_recv,
    weight, weight_sem, head_out, outbox, inbox, middle, landed, pair_send, pair_recv, line_send, line_recv,
):
    slots, heads, tokens, nope = query_ref.shape
    latent, rope_width = up_ref.shape[2], rotary_ref.shape[2]
    width = value_ref.shape[2]
    groups = latent // rope_width
    span = cache_ref.shape[1] * groups // (groups + 1)
    rows = heads * tokens
    half = lax.axis_size("head") // 2
    me = lax.axis_index("head")
    mine, odd = me // 2, me % 2
    partner, right, left = me + 1 - 2 * odd, me + 2, me - 2
    group = lax.axis_index("req")
    not_first, not_last = mine > 0, mine < half - 1

    barrier = pltpu.get_barrier_semaphore()
    pl.semaphore_signal(barrier, inc=1, device_id={"req": 1 - group}, device_id_type=MESH)
    pl.semaphore_signal(barrier, inc=1, device_id={"head": partner}, device_id_type=MESH)

    for i in range(1, half):
        peer = lax.rem(mine + i, half) * 2 + odd
        pl.semaphore_signal(barrier, inc=1, device_id={"head": peer}, device_id_type=MESH)
    pl.semaphore_wait(barrier, half + 1)

    def swap():
        return pltpu.make_async_remote_copy(
            src_ref=cache_ref, dst_ref=both.at[group], send_sem=swap_send, recv_sem=swap_recv,
            device_id={"req": 1 - group}, device_id_type=MESH,
        )

    def swap_in():
        return pltpu.make_async_remote_copy(
            src_ref=cache_ref, dst_ref=both.at[1 - group], send_sem=swap_send, recv_sem=swap_recv,
            device_id={"req": 1 - group}, device_id_type=MESH,
        )

    def to_partner(source, target, send, recv, slot):
        return pltpu.make_async_remote_copy(
            src_ref=source, dst_ref=target, send_sem=send.at[slot], recv_sem=recv.at[slot],
            device_id={"head": partner}, device_id_type=MESH,
        )

    def send_query(slot):
        return to_partner(full.at[slot, 0], full.at[slot, 1], query_send, query_recv, slot)

    def send_partial(slot):
        return to_partner(partial.at[slot], partial_in.at[slot], partial_send, partial_recv, slot)

    def send_stats(slot):
        return to_partner(stats.at[slot], stats_in.at[slot], stats_send, stats_recv, slot)

    def along(slot, step, block, send, recv, device):
        return pltpu.make_async_remote_copy(
            src_ref=blocks.at[slot, block], dst_ref=blocks.at[slot, block],
            send_sem=send.at[slot, step], recv_sem=recv.at[slot, step],
            device_id={"head": device}, device_id_type=MESH,
        )

    def rightward(slot, step, block):
        return along(slot, step, block, right_send, right_recv, right)

    def leftward(slot, step, block):
        return along(slot, step, block, left_send, left_recv, left)

    def send_right(slot, step):
        @pl.when(not_last & (mine - step >= 0))
        def _():
            rightward(slot, step, mine - step).start()

    def send_left(slot, step):
        @pl.when(not_first & (mine + step < half))
        def _():
            leftward(slot, step, mine + step).start()

    def load_weight():
        return pltpu.make_async_copy(weight_hbm, weight, weight_sem)

    per = tokens // (2 * half)
    pieces, chunks, chunk = middle.shape[3] // per, middle.shape[1], middle.shape[4]

    def columns(c, piece):
        start = piece * chunks * chunk + c * chunk
        return slice(start, start + chunk)

    def send_pair(slot, c):
        return pltpu.make_async_remote_copy(
            src_ref=outbox.at[slot, c], dst_ref=inbox.at[slot, c],
            send_sem=pair_send.at[slot, c], recv_sem=pair_recv.at[slot, c],
            device_id={"head": partner}, device_id_type=MESH,
        )

    def send_line(slot, c, i):
        k = lax.rem(mine + i, half)
        return pltpu.make_async_remote_copy(
            src_ref=middle.at[slot, c, k], dst_ref=landed.at[slot, c, i],
            send_sem=line_send.at[slot, c, i], recv_sem=line_recv.at[slot, c, i],
            device_id={"head": k * 2 + odd}, device_id_type=MESH,
        )

    def project_partner(slot):
        lines = head_out[slot, 1 - odd]
        for c in range(chunks):
            for piece in range(pieces):
                outbox[slot, c, :, piece * chunk:(piece + 1) * chunk] = jnp.dot(
                    lines, weight[:, columns(c, piece)], preferred_element_type=F32
                ).astype(BF16)
            send_pair(slot, c).start()

    def project_mine(slot):
        lines = head_out[slot, odd]
        for c in range(chunks):
            products = [
                jnp.dot(lines, weight[:, columns(c, piece)], preferred_element_type=F32)
                for piece in range(pieces)
            ]
            send_pair(slot, c).wait_recv()
            arrived = inbox[slot, c].astype(F32)
            sums = [
                products[piece] + arrived[:, piece * chunk:(piece + 1) * chunk] for piece in range(pieces)
            ]
            for k in range(half):
                middle[slot, c, k] = jnp.concatenate(
                    [part[k * per:(k + 1) * per] for part in sums], axis=0
                ).astype(BF16)
            for i in range(1, half):
                send_line(slot, c, i).start()

    swap().start()
    load_weight().start()
    both[group] = cache_ref[...]

    @pl.loop(0, slots)
    def _(slot):
        for h in range(heads):
            full[slot, 0, h * tokens:(h + 1) * tokens, :latent] = jnp.dot(
                query_ref[slot, h], up_ref[h], preferred_element_type=F32
            ).astype(BF16)
        full[slot, 0, :, latent:latent + rope_width] = rotary_ref[slot]
        full[slot, 0, :, latent + rope_width:] = jnp.zeros(
            (rows, full.shape[3] - latent - rope_width), BF16
        )
        send_query(slot).start()

    swap_in().wait_recv()

    @pl.loop(0, slots)
    def _(slot):
        request = request_ref[group * slots + slot]
        blocks[slot, mine] = both[request // slots, request % slots]

    for slot in range(min(2, slots)):
        send_right(slot, 0)
        send_left(slot, 0)

    generated = own_mask(2 * rows, steps, cont, per)
    generated = generated & (lax.broadcasted_iota(jnp.int32, generated.shape, 0) < rows)

    def merge(slot):
        send_partial(slot).wait_recv()
        send_stats(slot).wait_recv()
        other_top, other_total = stats_in[slot, :, :1], stats_in[slot, :, 64:65]
        top = jnp.maximum(kept_top[slot], other_top)
        here = jnp.exp(kept_top[slot] - top)
        there = jnp.exp(other_top - top) * other_total
        total = kept_total[slot] * here + there
        attended = (kept[slot] * here + partial_in[slot].astype(F32) * there) / total
        attended = attended.astype(BF16)
        for h in range(heads):
            values = jnp.dot(
                attended[h * tokens:(h + 1) * tokens], value_ref[h], preferred_element_type=F32
            ).astype(BF16)
            head_out[slot, 0, :, h * width:(h + 1) * width] = values[:tokens // 2]
            head_out[slot, 1, :, h * width:(h + 1) * width] = values[tokens // 2:]

    @pl.loop(0, slots)
    def _(slot):
        length = length_ref[request_ref[group * slots + slot]]

        def absorb(block):
            keys = blocks[slot, block, :span]
            packed = blocks[slot, block, span:]
            rope = jnp.concatenate(
                [packed[:, g * rope_width:(g + 1) * rope_width] for g in range(groups)], axis=0
            )
            stripe = block * 2 + odd
            place = stripe * span + lax.broadcasted_iota(jnp.int32, (2 * rows, span), 1)
            query = full[slot].reshape(2 * rows, full.shape[3])
            state = attend(
                (top_ref[...], total_ref[...], acc_ref[...]),
                query[:, :latent], query[:, latent:latent + rope_width], keys, rope,
                place < length, scale,
            )
            top_ref[...], total_ref[...], acc_ref[...] = state

        send_query(slot).wait_recv()
        query = full[slot].reshape(2 * rows, full.shape[3])
        own = own_ref[slot]
        zero = (
            jnp.full((2 * rows, 1), LOW, F32),
            jnp.zeros((2 * rows, 1), F32),
            jnp.zeros((2 * rows, latent), F32),
        )
        state = attend(
            zero, query[:, :latent], query[:, latent:latent + rope_width],
            own[:, :latent], own[:, latent:], generated, scale,
        )
        top_ref[...], total_ref[...], acc_ref[...] = state
        absorb(mine)

        @pl.when(slot == 1)
        def _():
            load_weight().wait()

        @pl.when(slot > 0)
        def _():
            merge(slot - 1)
            project_partner(slot - 1)

        for step in range(half - 1):
            from_left, from_right = mine - 1 - step >= 0, mine + 1 + step < half

            @pl.when(from_left)
            def _():
                rightward(slot, step, mine - 1 - step).wait_recv()

            if step + 1 < half - 1:
                send_right(slot, step + 1)

            @pl.when(from_right)
            def _():
                leftward(slot, step, mine + 1 + step).wait_recv()

            if step + 1 < half - 1:
                send_left(slot, step + 1)

            @pl.when(from_left)
            def _():
                absorb(mine - 1 - step)

            @pl.when(from_right)
            def _():
                absorb(mine + 1 + step)

        @pl.when(slot + 2 < slots)
        def _():
            send_right(slot + 2, 0)
            send_left(slot + 2, 0)

        total = total_ref[rows:]
        partial[slot] = (acc_ref[rows:] / jnp.where(total > 0.0, total, 1.0)).astype(BF16)
        lane = lax.broadcasted_iota(jnp.int32, (rows, 128), 1)
        stats[slot] = jnp.where(lane < 64, top_ref[rows:], total)
        send_partial(slot).start()
        send_stats(slot).start()
        kept[slot] = acc_ref[:rows]
        kept_top[slot] = top_ref[:rows]
        kept_total[slot] = total_ref[:rows]

        @pl.when(slot > 0)
        def _():
            project_mine(slot - 1)

    merge(slots - 1)
    project_partner(slots - 1)
    project_mine(slots - 1)

    @pl.loop(0, slots)
    def _(slot):
        for c in range(chunks):
            total = middle[slot, c, mine].astype(F32)
            for i in range(1, half):
                send_line(slot, c, i).wait_recv()
                total = total + landed[slot, c, i].astype(F32)
            out_ref[slot, :, c * chunk:(c + 1) * chunk] = total.astype(BF16)

    swap().wait_send()

    @pl.loop(0, slots)
    def _(slot):
        send_query(slot).wait_send()
        send_partial(slot).wait_send()
        send_stats(slot).wait_send()
        for c in range(chunks):
            send_pair(slot, c).wait_send()
            for i in range(1, half):
                send_line(slot, c, i).wait_send()
        for step in range(half - 1):
            @pl.when(not_last & (mine - step >= 0))
            def _():
                rightward(slot, step, mine - step).wait_send()

            @pl.when(not_first & (mine + step < half))
            def _():
                leftward(slot, step, mine + step).wait_send()


def shards(
    latent_cache, lengths, slot_request, queries, new_latent, key_up, value_up, output_weight
):
    slots, span, cache_width = latent_cache.shape
    nope, latent = key_up.shape[1], key_up.shape[2]
    steps, _, cont, heads, query_width = queries.shape
    vhead = value_up.shape[2]
    tokens = steps * cont
    rows = tokens * heads
    scale = (nope + cache_width - latent) ** (-0.5)
    stripes, groups = lax.axis_size("head"), lax.axis_size("req")
    half = stripes // 2
    per = tokens // stripes
    pieces = max(1, 16 // per)
    depth, out_width = heads * vhead, output_weight.shape[2]
    reach = out_width // pieces
    chunk = 896 if reach % 896 == 0 else reach
    chunks = reach // chunk
    rope = cache_width - latent
    packs = latent // rope
    query_rows = jnp.transpose(queries, (1, 3, 0, 2, 4)).reshape(slots, heads, half, 2, per, query_width)
    query_rows = jnp.transpose(query_rows, (0, 1, 3, 2, 4, 5)).reshape(slots, heads, tokens, query_width)
    rotary_rows = query_rows[..., nope:].reshape(slots, rows, rope)
    own_rows = jnp.transpose(new_latent, (1, 0, 2, 3)).reshape(slots, tokens, cache_width)
    packed = latent_cache[..., latent:].reshape(slots, packs, span // packs, rope)
    packed = jnp.transpose(packed, (0, 2, 1, 3)).reshape(slots, span // packs, latent)
    cache_rows = jnp.concatenate([latent_cache[..., :latent], packed], axis=1)
    deep = span + span // packs
    vmem, smem = pl.BlockSpec(memory_space=pltpu.VMEM), pl.BlockSpec(memory_space=pltpu.SMEM)
    padded = -(-cache_width // 128) * 128
    dma = pltpu.SemaphoreType.DMA
    summed = pl.pallas_call(
        functools.partial(attention_kernel, scale, steps, cont),
        out_shape=jax.ShapeDtypeStruct((slots, pieces * per, reach), BF16),
        in_specs=[smem, smem] + [vmem] * 6 + [pl.BlockSpec(memory_space=pl.ANY)],
        out_specs=vmem,
        scratch_shapes=[
            pltpu.VMEM((groups, slots, deep, latent), BF16),
            pltpu.VMEM((slots, half, deep, latent), BF16),
            pltpu.VMEM((slots, 2, rows, padded), BF16),
            pltpu.VMEM((2 * rows, 1), F32),
            pltpu.VMEM((2 * rows, 1), F32),
            pltpu.VMEM((2 * rows, latent), F32),
            pltpu.VMEM((slots, rows, latent), F32),
            pltpu.VMEM((slots, rows, 1), F32),
            pltpu.VMEM((slots, rows, 1), F32),
            pltpu.VMEM((slots, rows, latent), BF16),
            pltpu.VMEM((slots, rows, latent), BF16),
            pltpu.VMEM((slots, rows, 128), F32),
            pltpu.VMEM((slots, rows, 128), F32),
            dma, dma, dma((slots,)), dma((slots,)),
            dma((slots, half - 1)), dma((slots, half - 1)), dma((slots, half - 1)), dma((slots, half - 1)),
            dma((slots,)), dma((slots,)), dma((slots,)), dma((slots,)),
            pltpu.VMEM((depth, out_width), BF16),
            dma,
            pltpu.VMEM((slots, 2, tokens // 2, depth), BF16),
            pltpu.VMEM((slots, chunks, half * per, pieces * chunk), BF16),
            pltpu.VMEM((slots, chunks, half * per, pieces * chunk), BF16),
            pltpu.VMEM((slots, chunks, half, pieces * per, chunk), BF16),
            pltpu.VMEM((slots, chunks, half, pieces * per, chunk), BF16),
            dma((slots, chunks)), dma((slots, chunks)),
            dma((slots, chunks, half)), dma((slots, chunks, half)),
        ],
        compiler_params=pltpu.CompilerParams(
            collective_id=2, has_side_effects=True, vmem_limit_bytes=48 * 1024 * 1024
        ),
        cost_estimate=pl.CostEstimate(
            flops=4 * slots * rows * stripes * span * latent,
            bytes_accessed=2 * slots * deep * latent,
            transcendentals=slots * rows * stripes * span,
        ),
    )(slot_request, lengths, cache_rows, query_rows[..., :nope], rotary_rows, own_rows, key_up, value_up,
      output_weight.reshape(depth, out_width))
    summed = jnp.transpose(summed.reshape(slots, pieces, per, reach), (2, 0, 1, 3))
    return summed.reshape(per, slots, out_width)


def solution(mesh):
    in_specs = (
        P(("parts", "req"), "head", None),
        P("parts"),
        P("parts"),
        P(None, ("parts", "req"), None, "head", None),
        P(None, ("parts", "req"), None, None),
        P("head", None, None),
        P("head", None, None),
        P("head", None, None),
    )
    out_specs = P("head", ("parts", "req"), None)
    return jax.shard_map(shards, mesh=mesh, in_specs=in_specs, out_specs=out_specs, check_vma=False)
```

```python
import functools

import jax
import jax.numpy as jnp
from jax import lax
from jax.experimental import pallas as pl
from jax.experimental.pallas import tpu as pltpu
from jax.sharding import PartitionSpec as P

MESH = pl.DeviceIdType.MESH
F32 = jnp.float32
BF16 = jnp.bfloat16
LOW = -1e30


def dot_nt(a, b):
    return lax.dot_general(a, b, (((1,), (1,)), ((), ())), preferred_element_type=F32)


def attend(state, absorbed, rotary, keys, rope, mask, scale):
    top, total, acc = state
    scores = (dot_nt(absorbed, keys) + dot_nt(rotary, rope)) * scale
    scores = jnp.where(mask, scores, LOW)
    new_top = jnp.maximum(top, jnp.max(scores, axis=1, keepdims=True))
    weights = jnp.exp(scores - new_top)
    rescale = jnp.exp(top - new_top)
    total = total * rescale + jnp.sum(weights, axis=1, keepdims=True)
    acc = acc * rescale + jnp.dot(weights.astype(BF16), keys, preferred_element_type=F32)
    return new_top, total, acc


def own_mask(rows, steps, cont, per):
    tokens = steps * cont
    row = lax.broadcasted_iota(jnp.int32, (rows, tokens), 0) % tokens
    odd, rest = row // (tokens // 2), row % (tokens // 2)
    row = (2 * (rest // per) + odd) * per + rest % per
    col = lax.broadcasted_iota(jnp.int32, (rows, tokens), 1)
    return (row % cont == col % cont) & (col // cont <= row // cont)


def attention_kernel(
    scale, steps, cont,
    request_ref, length_ref, cache_ref, query_ref, rotary_ref, own_ref, up_ref, value_ref, weight_hbm, out_ref,
    both, blocks, full, top_ref, total_ref, acc_ref, kept, kept_top, kept_total,
    partial, partial_in, stats, stats_in,
    swap_send, swap_recv, query_send, query_recv, right_send, right_recv, left_send, left_recv,
    partial_send, partial_recv, stats_send, stats_recv,
    weight, weight_sem, head_out, outbox, inbox, middle, landed, pair_send, pair_recv, line_send, line_recv,
):
    slots, heads, tokens, nope = query_ref.shape
    latent, rope_width = up_ref.shape[2], rotary_ref.shape[2]
    width = value_ref.shape[2]
    groups = latent // rope_width
    span = cache_ref.shape[1]
    share = span // groups
    rows = heads * tokens
    half = lax.axis_size("head") // 2
    me = lax.axis_index("head")
    mine, odd = me // 2, me % 2
    partner, right, left = me + 1 - 2 * odd, me + 2, me - 2
    group = lax.axis_index("req")
    not_first, not_last = mine > 0, mine < half - 1

    for slot in range(slots):
        both[group, slot, :span] = cache_ref[slot, :, :latent]
        both[group, slot, span:] = jnp.concatenate(
            [cache_ref[slot, g * share:(g + 1) * share, latent:] for g in range(groups)], axis=1
        )

    barrier = pltpu.get_barrier_semaphore()
    pl.semaphore_signal(barrier, inc=1, device_id={"req": 1 - group}, device_id_type=MESH)
    pl.semaphore_signal(barrier, inc=1, device_id={"head": partner}, device_id_type=MESH)

    for i in range(1, half):
        peer = lax.rem(mine + i, half) * 2 + odd
        pl.semaphore_signal(barrier, inc=1, device_id={"head": peer}, device_id_type=MESH)
    pl.semaphore_wait(barrier, half + 1)

    def swap():
        return pltpu.make_async_remote_copy(
            src_ref=both.at[group], dst_ref=both.at[group], send_sem=swap_send, recv_sem=swap_recv,
            device_id={"req": 1 - group}, device_id_type=MESH,
        )

    def swap_in():
        return pltpu.make_async_remote_copy(
            src_ref=both.at[group], dst_ref=both.at[1 - group], send_sem=swap_send, recv_sem=swap_recv,
            device_id={"req": 1 - group}, device_id_type=MESH,
        )

    def to_partner(source, target, send, recv, slot):
        return pltpu.make_async_remote_copy(
            src_ref=source, dst_ref=target, send_sem=send.at[slot], recv_sem=recv.at[slot],
            device_id={"head": partner}, device_id_type=MESH,
        )

    def send_query(slot):
        return to_partner(full.at[slot, 0], full.at[slot, 1], query_send, query_recv, slot)

    def send_partial(slot):
        return to_partner(partial.at[slot], partial_in.at[slot], partial_send, partial_recv, slot)

    def send_stats(slot):
        return to_partner(stats.at[slot], stats_in.at[slot], stats_send, stats_recv, slot)

    def along(slot, step, block, send, recv, device):
        return pltpu.make_async_remote_copy(
            src_ref=blocks.at[slot, block], dst_ref=blocks.at[slot, block],
            send_sem=send.at[slot, step], recv_sem=recv.at[slot, step],
            device_id={"head": device}, device_id_type=MESH,
        )

    def rightward(slot, step, block):
        return along(slot, step, block, right_send, right_recv, right)

    def leftward(slot, step, block):
        return along(slot, step, block, left_send, left_recv, left)

    def send_right(slot, step):
        @pl.when(not_last & (mine - step >= 0))
        def _():
            rightward(slot, step, mine - step).start()

    def send_left(slot, step):
        @pl.when(not_first & (mine + step < half))
        def _():
            leftward(slot, step, mine + step).start()

    def load_weight():
        return pltpu.make_async_copy(weight_hbm, weight, weight_sem)

    per = tokens // (2 * half)
    pieces, chunks, chunk = middle.shape[3] // per, middle.shape[1], middle.shape[4]

    def columns(c, piece):
        start = piece * chunks * chunk + c * chunk
        return slice(start, start + chunk)

    def send_pair(slot, c):
        return pltpu.make_async_remote_copy(
            src_ref=outbox.at[slot, c], dst_ref=inbox.at[slot, c],
            send_sem=pair_send.at[slot, c], recv_sem=pair_recv.at[slot, c],
            device_id={"head": partner}, device_id_type=MESH,
        )

    def send_line(slot, c, i):
        k = lax.rem(mine + i, half)
        return pltpu.make_async_remote_copy(
            src_ref=middle.at[slot, c, k], dst_ref=landed.at[slot, c, i],
            send_sem=line_send.at[slot, c, i], recv_sem=line_recv.at[slot, c, i],
            device_id={"head": k * 2 + odd}, device_id_type=MESH,
        )

    def project_partner(slot):
        lines = head_out[slot, 1 - odd]
        for c in range(chunks):
            for piece in range(pieces):
                outbox[slot, c, :, piece * chunk:(piece + 1) * chunk] = jnp.dot(
                    lines, weight[:, columns(c, piece)], preferred_element_type=F32
                ).astype(BF16)
            send_pair(slot, c).start()

    def project_mine(slot):
        lines = head_out[slot, odd]
        for c in range(chunks):
            products = [
                jnp.dot(lines, weight[:, columns(c, piece)], preferred_element_type=F32)
                for piece in range(pieces)
            ]
            send_pair(slot, c).wait_recv()
            arrived = inbox[slot, c].astype(F32)
            sums = [
                products[piece] + arrived[:, piece * chunk:(piece + 1) * chunk] for piece in range(pieces)
            ]
            for k in range(half):
                middle[slot, c, k] = jnp.concatenate(
                    [part[k * per:(k + 1) * per] for part in sums], axis=0
                ).astype(BF16)
            for i in range(1, half):
                send_line(slot, c, i).start()

    swap().start()
    load_weight().start()

    @pl.loop(0, slots)
    def _(slot):
        for h in range(heads):
            full[slot, 0, h * tokens:(h + 1) * tokens, :latent] = jnp.dot(
                query_ref[slot, h], up_ref[h], preferred_element_type=F32
            ).astype(BF16)
        full[slot, 0, :, latent:latent + rope_width] = rotary_ref[slot]
        full[slot, 0, :, latent + rope_width:] = jnp.zeros(
            (rows, full.shape[3] - latent - rope_width), BF16
        )
        send_query(slot).start()

    swap_in().wait_recv()

    @pl.loop(0, slots)
    def _(slot):
        request = request_ref[group * slots + slot]
        blocks[slot, mine] = both[request // slots, request % slots]

    for slot in range(min(2, slots)):
        send_right(slot, 0)
        send_left(slot, 0)

    generated = own_mask(2 * rows, steps, cont, per)
    generated = generated & (lax.broadcasted_iota(jnp.int32, generated.shape, 0) < rows)

    def merge(slot):
        send_partial(slot).wait_recv()
        send_stats(slot).wait_recv()
        other = jnp.transpose(stats_in[slot])
        other_top, other_total = other[:, :1], other[:, 1:2]
        top = jnp.maximum(kept_top[slot], other_top)
        here = jnp.exp(kept_top[slot] - top)
        there = jnp.exp(other_top - top) * other_total
        total = kept_total[slot] * here + there
        attended = (kept[slot] * here + partial_in[slot].astype(F32) * there) / total
        attended = attended.astype(BF16)
        for h in range(heads):
            values = jnp.dot(
                attended[h * tokens:(h + 1) * tokens], value_ref[h], preferred_element_type=F32
            ).astype(BF16)
            head_out[slot, 0, :, h * width:(h + 1) * width] = values[:tokens // 2]
            head_out[slot, 1, :, h * width:(h + 1) * width] = values[tokens // 2:]

    @pl.loop(0, slots)
    def _(slot):
        length = length_ref[request_ref[group * slots + slot]]

        def absorb(block):
            keys = blocks[slot, block, :span]
            packed = blocks[slot, block, span:]
            rope = jnp.concatenate(
                [packed[:, g * rope_width:(g + 1) * rope_width] for g in range(groups)], axis=0
            )
            stripe = block * 2 + odd
            place = stripe * span + lax.broadcasted_iota(jnp.int32, (2 * rows, span), 1)
            query = full[slot].reshape(2 * rows, full.shape[3])
            state = attend(
                (top_ref[...], total_ref[...], acc_ref[...]),
                query[:, :latent], query[:, latent:latent + rope_width], keys, rope,
                place < length, scale,
            )
            top_ref[...], total_ref[...], acc_ref[...] = state

        send_query(slot).wait_recv()
        query = full[slot].reshape(2 * rows, full.shape[3])
        own = own_ref[slot]
        zero = (
            jnp.full((2 * rows, 1), 0.5 * LOW, F32),
            jnp.zeros((2 * rows, 1), F32),
            jnp.zeros((2 * rows, latent), F32),
        )
        state = attend(
            zero, query[:, :latent], query[:, latent:latent + rope_width],
            own[:, :latent], own[:, latent:], generated, scale,
        )
        top_ref[...], total_ref[...], acc_ref[...] = state
        absorb(mine)

        @pl.when(slot == 1)
        def _():
            load_weight().wait()

        @pl.when(slot > 0)
        def _():
            merge(slot - 1)
            project_partner(slot - 1)

        for step in range(half - 1):
            from_left, from_right = mine - 1 - step >= 0, mine + 1 + step < half

            @pl.when(from_left)
            def _():
                rightward(slot, step, mine - 1 - step).wait_recv()

            if step + 1 < half - 1:
                send_right(slot, step + 1)

            @pl.when(from_right)
            def _():
                leftward(slot, step, mine + 1 + step).wait_recv()

            if step + 1 < half - 1:
                send_left(slot, step + 1)

            @pl.when(from_left)
            def _():
                absorb(mine - 1 - step)

            @pl.when(from_right)
            def _():
                absorb(mine + 1 + step)

        @pl.when(slot + 2 < slots)
        def _():
            send_right(slot + 2, 0)
            send_left(slot + 2, 0)

        total = total_ref[rows:]
        partial[slot] = (acc_ref[rows:] / jnp.where(total > 0.0, total, 1.0)).astype(BF16)
        lane = lax.broadcasted_iota(jnp.int32, (rows, 128), 1)
        stats[slot] = jnp.transpose(jnp.where(lane % 2 == 0, top_ref[rows:], total))[:8]
        send_partial(slot).start()
        send_stats(slot).start()
        kept[slot] = acc_ref[:rows]
        kept_top[slot] = top_ref[:rows]
        kept_total[slot] = total_ref[:rows]

        @pl.when(slot > 0)
        def _():
            project_mine(slot - 1)

    merge(slots - 1)
    project_partner(slots - 1)
    project_mine(slots - 1)

    @pl.loop(0, slots)
    def _(slot):
        for c in range(chunks):
            total = middle[slot, c, mine].astype(F32)
            for i in range(1, half):
                send_line(slot, c, i).wait_recv()
                total = total + landed[slot, c, i].astype(F32)
            out_ref[slot, :, c * chunk:(c + 1) * chunk] = total.astype(BF16)

    swap().wait_send()

    @pl.loop(0, slots)
    def _(slot):
        send_query(slot).wait_send()
        send_partial(slot).wait_send()
        send_stats(slot).wait_send()
        for c in range(chunks):
            send_pair(slot, c).wait_send()
            for i in range(1, half):
                send_line(slot, c, i).wait_send()
        for step in range(half - 1):
            @pl.when(not_last & (mine - step >= 0))
            def _():
                rightward(slot, step, mine - step).wait_send()

            @pl.when(not_first & (mine + step < half))
            def _():
                leftward(slot, step, mine + step).wait_send()


def shards(
    latent_cache, lengths, slot_request, queries, new_latent, key_up, value_up, output_weight
):
    slots, span, cache_width = latent_cache.shape
    nope, latent = key_up.shape[1], key_up.shape[2]
    steps, _, cont, heads, query_width = queries.shape
    vhead = value_up.shape[2]
    tokens = steps * cont
    rows = tokens * heads
    scale = (nope + cache_width - latent) ** (-0.5)
    stripes, groups = lax.axis_size("head"), lax.axis_size("req")
    half = stripes // 2
    per = tokens // stripes
    pieces = max(1, 16 // per)
    depth, out_width = heads * vhead, output_weight.shape[2]
    reach = out_width // pieces
    chunk = 896 if reach % 896 == 0 else reach
    chunks = reach // chunk
    rope = cache_width - latent
    packs = latent // rope
    query_rows = jnp.transpose(queries, (1, 3, 0, 2, 4)).reshape(slots, heads, half, 2, per, query_width)
    query_rows = jnp.transpose(query_rows, (0, 1, 3, 2, 4, 5)).reshape(slots, heads, tokens, query_width)
    rotary_rows = query_rows[..., nope:].reshape(slots, rows, rope)
    own_rows = jnp.transpose(new_latent, (1, 0, 2, 3)).reshape(slots, tokens, cache_width)
    deep = span + span // packs
    vmem, smem = pl.BlockSpec(memory_space=pltpu.VMEM), pl.BlockSpec(memory_space=pltpu.SMEM)
    padded = -(-cache_width // 128) * 128
    dma = pltpu.SemaphoreType.DMA
    summed = pl.pallas_call(
        functools.partial(attention_kernel, scale, steps, cont),
        out_shape=jax.ShapeDtypeStruct((slots, pieces * per, reach), BF16),
        in_specs=[smem, smem] + [vmem] * 6 + [pl.BlockSpec(memory_space=pl.ANY)],
        out_specs=vmem,
        scratch_shapes=[
            pltpu.VMEM((groups, slots, deep, latent), BF16),
            pltpu.VMEM((slots, half, deep, latent), BF16),
            pltpu.VMEM((slots, 2, rows, padded), BF16),
            pltpu.VMEM((2 * rows, 1), F32),
            pltpu.VMEM((2 * rows, 1), F32),
            pltpu.VMEM((2 * rows, latent), F32),
            pltpu.VMEM((slots, rows, latent), F32),
            pltpu.VMEM((slots, rows, 1), F32),
            pltpu.VMEM((slots, rows, 1), F32),
            pltpu.VMEM((slots, rows, latent), BF16),
            pltpu.VMEM((slots, rows, latent), BF16),
            pltpu.VMEM((slots, 8, rows), F32),
            pltpu.VMEM((slots, 8, rows), F32),
            dma, dma, dma((slots,)), dma((slots,)),
            dma((slots, half - 1)), dma((slots, half - 1)), dma((slots, half - 1)), dma((slots, half - 1)),
            dma((slots,)), dma((slots,)), dma((slots,)), dma((slots,)),
            pltpu.VMEM((depth, out_width), BF16),
            dma,
            pltpu.VMEM((slots, 2, tokens // 2, depth), BF16),
            pltpu.VMEM((slots, chunks, half * per, pieces * chunk), BF16),
            pltpu.VMEM((slots, chunks, half * per, pieces * chunk), BF16),
            pltpu.VMEM((slots, chunks, half, pieces * per, chunk), BF16),
            pltpu.VMEM((slots, chunks, half, pieces * per, chunk), BF16),
            dma((slots, chunks)), dma((slots, chunks)),
            dma((slots, chunks, half)), dma((slots, chunks, half)),
        ],
        compiler_params=pltpu.CompilerParams(
            collective_id=2, has_side_effects=True, vmem_limit_bytes=48 * 1024 * 1024
        ),
        cost_estimate=pl.CostEstimate(
            flops=4 * slots * rows * stripes * span * latent,
            bytes_accessed=2 * slots * deep * latent,
            transcendentals=slots * rows * stripes * span,
        ),
    )(slot_request, lengths, latent_cache, query_rows[..., :nope], rotary_rows, own_rows, key_up, value_up,
      output_weight.reshape(depth, out_width))
    summed = jnp.transpose(summed.reshape(slots, pieces, per, reach), (2, 0, 1, 3))
    return summed.reshape(per, slots, out_width)


def solution(mesh):
    in_specs = (
        P(("parts", "req"), "head", None),
        P("parts"),
        P("parts"),
        P(None, ("parts", "req"), None, "head", None),
        P(None, ("parts", "req"), None, None),
        P("head", None, None),
        P("head", None, None),
        P("head", None, None),
    )
    out_specs = P("head", ("parts", "req"), None)
    return jax.shard_map(shards, mesh=mesh, in_specs=in_specs, out_specs=out_specs, check_vma=False)
```

```python
import functools

import jax
import jax.numpy as jnp
from jax import lax
from jax.experimental import pallas as pl
from jax.experimental.pallas import tpu as pltpu
from jax.sharding import PartitionSpec as P

MESH = pl.DeviceIdType.MESH
F32 = jnp.float32
BF16 = jnp.bfloat16
LOW = -1e30


def dot_nt(a, b):
    return lax.dot_general(a, b, (((1,), (1,)), ((), ())), preferred_element_type=F32)


def attend(state, absorbed, rotary, keys, rope, mask, scale):
    top, total, acc = state
    scores = (dot_nt(absorbed, keys) + dot_nt(rotary, rope)) * scale
    scores = jnp.where(mask, scores, LOW)
    new_top = jnp.maximum(top, jnp.max(scores, axis=1, keepdims=True))
    weights = jnp.exp(scores - new_top)
    rescale = jnp.exp(top - new_top)
    total = total * rescale + jnp.sum(weights, axis=1, keepdims=True)
    acc = acc * rescale + jnp.dot(weights.astype(BF16), keys, preferred_element_type=F32)
    return new_top, total, acc


def own_mask(rows, steps, cont, per):
    tokens = steps * cont
    row = lax.broadcasted_iota(jnp.int32, (rows, tokens), 0) % tokens
    odd, rest = row // (tokens // 2), row % (tokens // 2)
    row = (2 * (rest // per) + odd) * per + rest % per
    col = lax.broadcasted_iota(jnp.int32, (rows, tokens), 1)
    return (row % cont == col % cont) & (col // cont <= row // cont)


def attention_kernel(
    scale, steps, cont,
    request_ref, length_ref, cache_ref, query_ref, rotary_ref, own_ref, up_ref, value_ref, weight_hbm, out_ref,
    both, blocks, full, top_ref, total_ref, acc_ref, kept, kept_top, kept_total,
    partial, partial_in, stats, stats_in,
    swap_send, swap_recv, query_send, query_recv, right_send, right_recv, left_send, left_recv,
    partial_send, partial_recv, stats_send, stats_recv,
    weight, weight_sem, head_out, outbox, inbox, middle, landed, pair_send, pair_recv, line_send, line_recv,
):
    slots, heads, tokens, nope = query_ref.shape
    latent, rope_width = up_ref.shape[2], rotary_ref.shape[2]
    width = value_ref.shape[2]
    groups = latent // rope_width
    span = cache_ref.shape[1]
    share = span // groups
    rows = heads * tokens
    half = lax.axis_size("head") // 2
    me = lax.axis_index("head")
    mine, odd = me // 2, me % 2
    partner, right, left = me + 1 - 2 * odd, me + 2, me - 2
    group = lax.axis_index("req")
    not_first, not_last = mine > 0, mine < half - 1

    for slot in range(slots):
        both[group, slot, :span] = cache_ref[slot, :, :latent]
        both[group, slot, span:] = jnp.concatenate(
            [cache_ref[slot, g * share:(g + 1) * share, latent:] for g in range(groups)], axis=1
        )

    barrier = pltpu.get_barrier_semaphore()
    pl.semaphore_signal(barrier, inc=1, device_id={"req": 1 - group}, device_id_type=MESH)
    pl.semaphore_signal(barrier, inc=1, device_id={"head": partner}, device_id_type=MESH)

    for i in range(1, half):
        peer = lax.rem(mine + i, half) * 2 + odd
        pl.semaphore_signal(barrier, inc=1, device_id={"head": peer}, device_id_type=MESH)
    pl.semaphore_wait(barrier, half + 1)

    def swap():
        return pltpu.make_async_remote_copy(
            src_ref=both.at[group], dst_ref=both.at[group], send_sem=swap_send, recv_sem=swap_recv,
            device_id={"req": 1 - group}, device_id_type=MESH,
        )

    def swap_in():
        return pltpu.make_async_remote_copy(
            src_ref=both.at[group], dst_ref=both.at[1 - group], send_sem=swap_send, recv_sem=swap_recv,
            device_id={"req": 1 - group}, device_id_type=MESH,
        )

    def to_partner(source, target, send, recv, slot):
        return pltpu.make_async_remote_copy(
            src_ref=source, dst_ref=target, send_sem=send.at[slot], recv_sem=recv.at[slot],
            device_id={"head": partner}, device_id_type=MESH,
        )

    def send_query(slot):
        return to_partner(full.at[slot, 0], full.at[slot, 1], query_send, query_recv, slot)

    def send_partial(slot):
        return to_partner(partial.at[slot], partial_in.at[slot], partial_send, partial_recv, slot)

    def send_stats(slot):
        return to_partner(stats.at[slot], stats_in.at[slot], stats_send, stats_recv, slot)

    def along(slot, step, block, send, recv, device):
        return pltpu.make_async_remote_copy(
            src_ref=blocks.at[slot, block], dst_ref=blocks.at[slot, block],
            send_sem=send.at[slot, step], recv_sem=recv.at[slot, step],
            device_id={"head": device}, device_id_type=MESH,
        )

    def rightward(slot, step, block):
        return along(slot, step, block, right_send, right_recv, right)

    def leftward(slot, step, block):
        return along(slot, step, block, left_send, left_recv, left)

    def send_right(slot, step):
        @pl.when(not_last & (mine - step >= 0))
        def _():
            rightward(slot, step, mine - step).start()

    def send_left(slot, step):
        @pl.when(not_first & (mine + step < half))
        def _():
            leftward(slot, step, mine + step).start()

    def load_weight():
        return pltpu.make_async_copy(weight_hbm, weight, weight_sem)

    per = tokens // (2 * half)
    pieces, chunks, chunk = middle.shape[3] // per, middle.shape[1], middle.shape[4]

    def columns(c, piece):
        start = piece * chunks * chunk + c * chunk
        return slice(start, start + chunk)

    def send_pair(slot, c):
        return pltpu.make_async_remote_copy(
            src_ref=outbox.at[slot, c], dst_ref=inbox.at[slot, c],
            send_sem=pair_send.at[slot, c], recv_sem=pair_recv.at[slot, c],
            device_id={"head": partner}, device_id_type=MESH,
        )

    def send_line(slot, c, i):
        k = lax.rem(mine + i, half)
        return pltpu.make_async_remote_copy(
            src_ref=middle.at[slot, c, k], dst_ref=landed.at[slot, c, i],
            send_sem=line_send.at[slot, c, i], recv_sem=line_recv.at[slot, c, i],
            device_id={"head": k * 2 + odd}, device_id_type=MESH,
        )

    def project_partner(slot):
        lines = head_out[slot, 1 - odd]
        for c in range(chunks):
            for piece in range(pieces):
                outbox[slot, c, :, piece * chunk:(piece + 1) * chunk] = jnp.dot(
                    lines, weight[:, columns(c, piece)], preferred_element_type=F32
                ).astype(BF16)
            send_pair(slot, c).start()

    def project_mine(slot):
        lines = head_out[slot, odd]
        for c in range(chunks):
            products = [
                jnp.dot(lines, weight[:, columns(c, piece)], preferred_element_type=F32)
                for piece in range(pieces)
            ]
            send_pair(slot, c).wait_recv()
            arrived = inbox[slot, c].astype(F32)
            sums = [
                products[piece] + arrived[:, piece * chunk:(piece + 1) * chunk] for piece in range(pieces)
            ]
            for k in range(half):
                middle[slot, c, k] = jnp.concatenate(
                    [part[k * per:(k + 1) * per] for part in sums], axis=0
                ).astype(BF16)
            for i in range(1, half):
                send_line(slot, c, i).start()

    swap().start()
    load_weight().start()

    @pl.loop(0, slots)
    def _(slot):
        for h in range(heads):
            full[slot, 0, h * tokens:(h + 1) * tokens, :latent] = jnp.dot(
                query_ref[slot, h], up_ref[h], preferred_element_type=F32
            ).astype(BF16)
        full[slot, 0, :, latent:latent + rope_width] = rotary_ref[slot]
        full[slot, 0, :, latent + rope_width:] = jnp.zeros(
            (rows, full.shape[3] - latent - rope_width), BF16
        )
        send_query(slot).start()

    swap_in().wait_recv()

    @pl.loop(0, slots)
    def _(slot):
        request = request_ref[group * slots + slot]
        blocks[slot, mine] = both[request // slots, request % slots]

    for slot in range(min(2, slots)):
        send_right(slot, 0)
        send_left(slot, 0)

    generated = own_mask(2 * rows, steps, cont, per)
    generated = generated & (lax.broadcasted_iota(jnp.int32, generated.shape, 0) < rows)

    def merge(slot):
        send_partial(slot).wait_recv()
        send_stats(slot).wait_recv()
        other = jnp.transpose(stats_in[slot])
        other_top, other_total = other[:, :1], other[:, 1:2]
        top = jnp.maximum(kept_top[slot], other_top)
        here = jnp.exp(kept_top[slot] - top)
        there = jnp.exp(other_top - top) * other_total
        total = kept_total[slot] * here + there
        attended = (kept[slot] * here + partial_in[slot].astype(F32) * there) / total
        attended = attended.astype(BF16)
        for h in range(heads):
            values = jnp.dot(
                attended[h * tokens:(h + 1) * tokens], value_ref[h], preferred_element_type=F32
            ).astype(BF16)
            head_out[slot, 0, :, h * width:(h + 1) * width] = values[:tokens // 2]
            head_out[slot, 1, :, h * width:(h + 1) * width] = values[tokens // 2:]

    @pl.loop(0, slots)
    def _(slot):
        length = length_ref[request_ref[group * slots + slot]]

        def absorb(block):
            keys = blocks[slot, block, :span]
            packed = blocks[slot, block, span:]
            rope = jnp.concatenate(
                [packed[:, g * rope_width:(g + 1) * rope_width] for g in range(groups)], axis=0
            )
            stripe = block * 2 + odd
            place = stripe * span + lax.broadcasted_iota(jnp.int32, (2 * rows, span), 1)
            query = full[slot].reshape(2 * rows, full.shape[3])
            state = attend(
                (top_ref[...], total_ref[...], acc_ref[...]),
                query[:, :latent], query[:, latent:latent + rope_width], keys, rope,
                place < length, scale,
            )
            top_ref[...], total_ref[...], acc_ref[...] = state

        send_query(slot).wait_recv()
        query = full[slot].reshape(2 * rows, full.shape[3])
        own = own_ref[slot]
        zero = (
            jnp.full((2 * rows, 1), 0.5 * LOW, F32),
            jnp.zeros((2 * rows, 1), F32),
            jnp.zeros((2 * rows, latent), F32),
        )
        state = attend(
            zero, query[:, :latent], query[:, latent:latent + rope_width],
            own[:, :latent], own[:, latent:], generated, scale,
        )
        top_ref[...], total_ref[...], acc_ref[...] = state
        absorb(mine)

        @pl.when(slot == 1)
        def _():
            load_weight().wait()

        @pl.when(slot > 0)
        def _():
            merge(slot - 1)
            project_partner(slot - 1)

        for step in range(half - 1):
            from_left, from_right = mine - 1 - step >= 0, mine + 1 + step < half

            @pl.when(from_left)
            def _():
                rightward(slot, step, mine - 1 - step).wait_recv()

            if step + 1 < half - 1:
                send_right(slot, step + 1)

            @pl.when(from_right)
            def _():
                leftward(slot, step, mine + 1 + step).wait_recv()

            if step + 1 < half - 1:
                send_left(slot, step + 1)

            @pl.when(from_left)
            def _():
                absorb(mine - 1 - step)

            @pl.when(from_right)
            def _():
                absorb(mine + 1 + step)

        @pl.when(slot + 2 < slots)
        def _():
            send_right(slot + 2, 0)
            send_left(slot + 2, 0)

        total = total_ref[rows:]
        partial[slot] = (acc_ref[rows:] / jnp.where(total > 0.0, total, 1.0)).astype(BF16)
        lane = lax.broadcasted_iota(jnp.int32, (rows, 128), 1)
        stats[slot] = jnp.transpose(jnp.where(lane % 2 == 0, top_ref[rows:], total))[:8]
        send_partial(slot).start()
        send_stats(slot).start()
        kept[slot] = acc_ref[:rows]
        kept_top[slot] = top_ref[:rows]
        kept_total[slot] = total_ref[:rows]

        @pl.when(slot > 0)
        def _():
            project_mine(slot - 1)

    merge(slots - 1)
    project_partner(slots - 1)
    project_mine(slots - 1)

    @pl.loop(0, slots)
    def _(slot):
        for c in range(chunks):
            total = middle[slot, c, mine].astype(F32)
            for i in range(1, half):
                send_line(slot, c, i).wait_recv()
                total = total + landed[slot, c, i].astype(F32)
            out_ref[slot, :, c * chunk:(c + 1) * chunk] = total.astype(BF16)

    swap().wait_send()

    @pl.loop(0, slots)
    def _(slot):
        send_query(slot).wait_send()
        send_partial(slot).wait_send()
        send_stats(slot).wait_send()
        for c in range(chunks):
            send_pair(slot, c).wait_send()
            for i in range(1, half):
                send_line(slot, c, i).wait_send()
        for step in range(half - 1):
            @pl.when(not_last & (mine - step >= 0))
            def _():
                rightward(slot, step, mine - step).wait_send()

            @pl.when(not_first & (mine + step < half))
            def _():
                leftward(slot, step, mine + step).wait_send()


def shards(
    latent_cache, lengths, slot_request, queries, new_latent, key_up, value_up, output_weight
):
    slots, span, cache_width = latent_cache.shape
    nope, latent = key_up.shape[1], key_up.shape[2]
    steps, _, cont, heads, query_width = queries.shape
    vhead = value_up.shape[2]
    tokens = steps * cont
    rows = tokens * heads
    scale = (nope + cache_width - latent) ** (-0.5)
    stripes, groups = lax.axis_size("head"), lax.axis_size("req")
    half = stripes // 2
    per = tokens // stripes
    pieces = max(1, 16 // per)
    depth, out_width = heads * vhead, output_weight.shape[2]
    reach = out_width // pieces
    chunk = 1792 if reach % 1792 == 0 else reach
    chunks = reach // chunk
    rope = cache_width - latent
    packs = latent // rope
    query_rows = jnp.transpose(queries, (1, 3, 0, 2, 4)).reshape(slots, heads, half, 2, per, query_width)
    query_rows = jnp.transpose(query_rows, (0, 1, 3, 2, 4, 5)).reshape(slots, heads, tokens, query_width)
    rotary_rows = query_rows[..., nope:].reshape(slots, rows, rope)
    own_rows = jnp.transpose(new_latent, (1, 0, 2, 3)).reshape(slots, tokens, cache_width)
    deep = span + span // packs
    vmem, smem = pl.BlockSpec(memory_space=pltpu.VMEM), pl.BlockSpec(memory_space=pltpu.SMEM)
    padded = -(-cache_width // 128) * 128
    dma = pltpu.SemaphoreType.DMA
    summed = pl.pallas_call(
        functools.partial(attention_kernel, scale, steps, cont),
        out_shape=jax.ShapeDtypeStruct((slots, pieces * per, reach), BF16),
        in_specs=[smem, smem] + [vmem] * 6 + [pl.BlockSpec(memory_space=pl.ANY)],
        out_specs=vmem,
        scratch_shapes=[
            pltpu.VMEM((groups, slots, deep, latent), BF16),
            pltpu.VMEM((slots, half, deep, latent), BF16),
            pltpu.VMEM((slots, 2, rows, padded), BF16),
            pltpu.VMEM((2 * rows, 1), F32),
            pltpu.VMEM((2 * rows, 1), F32),
            pltpu.VMEM((2 * rows, latent), F32),
            pltpu.VMEM((slots, rows, latent), F32),
            pltpu.VMEM((slots, rows, 1), F32),
            pltpu.VMEM((slots, rows, 1), F32),
            pltpu.VMEM((slots, rows, latent), BF16),
            pltpu.VMEM((slots, rows, latent), BF16),
            pltpu.VMEM((slots, 8, rows), F32),
            pltpu.VMEM((slots, 8, rows), F32),
            dma, dma, dma((slots,)), dma((slots,)),
            dma((slots, half - 1)), dma((slots, half - 1)), dma((slots, half - 1)), dma((slots, half - 1)),
            dma((slots,)), dma((slots,)), dma((slots,)), dma((slots,)),
            pltpu.VMEM((depth, out_width), BF16),
            dma,
            pltpu.VMEM((slots, 2, tokens // 2, depth), BF16),
            pltpu.VMEM((slots, chunks, half * per, pieces * chunk), BF16),
            pltpu.VMEM((slots, chunks, half * per, pieces * chunk), BF16),
            pltpu.VMEM((slots, chunks, half, pieces * per, chunk), BF16),
            pltpu.VMEM((slots, chunks, half, pieces * per, chunk), BF16),
            dma((slots, chunks)), dma((slots, chunks)),
            dma((slots, chunks, half)), dma((slots, chunks, half)),
        ],
        compiler_params=pltpu.CompilerParams(
            collective_id=2, has_side_effects=True, vmem_limit_bytes=48 * 1024 * 1024
        ),
        cost_estimate=pl.CostEstimate(
            flops=4 * slots * rows * stripes * span * latent,
            bytes_accessed=2 * slots * deep * latent,
            transcendentals=slots * rows * stripes * span,
        ),
    )(slot_request, lengths, latent_cache, query_rows[..., :nope], rotary_rows, own_rows, key_up, value_up,
      output_weight.reshape(depth, out_width))
    summed = jnp.transpose(summed.reshape(slots, pieces, per, reach), (2, 0, 1, 3))
    return summed.reshape(per, slots, out_width)


def solution(mesh):
    in_specs = (
        P(("parts", "req"), "head", None),
        P("parts"),
        P("parts"),
        P(None, ("parts", "req"), None, "head", None),
        P(None, ("parts", "req"), None, None),
        P("head", None, None),
        P("head", None, None),
        P("head", None, None),
    )
    out_specs = P("head", ("parts", "req"), None)
    return jax.shard_map(shards, mesh=mesh, in_specs=in_specs, out_specs=out_specs, check_vma=False)
```
